128 devices in a mesh: grp: 16 (over y, z), tp: 8 (over x, core).
Axes of the slice: x: 4, y: 4, z: 4, core: 2. Of those that a mesh axis runs over, the one named last changes fastest.
Arguments:
- queries: bfloat16 [32, 8192], P(None, 'tp'), may hold values from -9 to 9, as said below
- cache_keys: bfloat16 [32, 16384, 1024], P(None, 'grp', 'tp'), may hold values from -6 to 6
- cache_values: bfloat16 [32, 16384, 1024], P(None, 'grp', 'tp'), may hold values from -6 to 6
- lengths: int32 [32], replicated, may hold values from 4096 to 16384, as said below
- new_keys: bfloat16 [16384, 1024], P('grp', 'tp'), may hold values from -6 to 6
- new_values: bfloat16 [16384, 1024], P('grp', 'tp'), may hold values from -6 to 6
- new_rows: int32 [16384], P('grp'), may hold values from 0 to 31
- owners: int32 [16384, 1], P('grp'), may hold values from 0 to 15; in each aligned block of 1024 rows (0 to 1023, 1024 to 2047, ...) at most 128 rows name the same one
- out_weight: bfloat16 [8192, 8192], P('tp', 'grp'), may hold values from -0.0625 to 0.0625
Outputs:
- mixed: bfloat16 [32, 8192], P(None, ('grp', 'tp'))
- pool_kv: bfloat16 [2, 32768, 1024], P(None, 'grp', 'tp')
The draws below stay inside these ranges and needn't reach their ends.
Inputs may be any that keep to these rules, and one draw needn't show every extreme that they name: In the hidden draw some queries may be far larger than typical ones. `lengths`: some sequence is exactly 16384 long. `owners`: within each aligned block of 1024 fresh tokens (those of one grp index) at most 128 name the same owner, a bound that some block reaches.
All inputs are finite; a program needn't handle non-finite values.
Results may differ from the reference program's by a relative error of at most 0.0048.
Values may be sent and summed in bfloat16 or wider, within the bound.
A program may use at most 64 MiB of HBM per device.

```python
import math
import jax
import jax.numpy as jnp
import numpy as np
from jax import lax

D = 8192
HEADS = 64
KV_HEADS = 8
HEAD_DIM = 128
ROWS = 32
NEW_DEV = 1024
KV_WIDTH = 1024
CONTEXT = 16384
SPAN = 16384
CAP = 128
POOL = 32768
N_GRP = 16


def draw_queries(key, part):
    key = jax.random.fold_in(key, 11)
    base = jnp.clip(jax.random.normal(key, (ROWS, D), jnp.float32), -6.0, 6.0)
    return base.astype(jnp.bfloat16)


def draw_cache_keys(key, part):
    key = jax.random.fold_in(key, 12)
    base = jnp.clip(jax.random.normal(key, (ROWS, CONTEXT, KV_WIDTH), jnp.float32), -6.0, 6.0)
    return base.astype(jnp.bfloat16)


def draw_lengths(key, part):
    key = jax.random.fold_in(key, 13)
    first_key, second_key = jax.random.split(key)
    drawn = jax.random.randint(first_key, (ROWS,), CONTEXT // 4, CONTEXT + 1, jnp.int32)
    longest = jax.random.randint(second_key, (), 0, ROWS, jnp.int32)
    return jnp.where(jnp.arange(ROWS, dtype=jnp.int32) == longest, CONTEXT, drawn).astype(jnp.int32)


def plant(array, own_key, smallest, high):
    extent = array.shape
    place = [jax.random.randint(jax.random.fold_in(own_key, axis), (), 0, extent[axis]) for axis in range(len(extent))]
    array = array.at[tuple(place)].set(smallest)
    longest = extent.index(max(extent))
    place[longest] = (place[longest] + 1) % extent[longest]
    return array.at[tuple(place)].set(high)


def level_of(key, dims, cuts, low, largest):
    level = 1.0
    for dim, shards_of in cuts:
        heights = jax.random.uniform(jax.random.fold_in(jax.random.fold_in(key, 6), dim), (shards_of,), jnp.float32, low / len(cuts), largest / len(cuts))
        level = level * jnp.repeat(jnp.exp(heights), dims[dim] // shards_of).reshape((-1,) + (1,) * (len(dims) - 1 - dim))
    return level


def assign_block(own_key, own, number, rows, count, top, bound, slope):
    ranking = jax.random.permutation(own_key, count)
    heavy_load, usual = shares(count, rows * top, bound, slope, True), shares(count, rows * top, bound, slope, False)
    places = jnp.arange(count)

    def named(sizes, rotation):
        used = int((sizes > 0).sum())
        fixed = max(1, used // 4)
        shifted = fixed + (places - fixed + rotation * (used - fixed)) % max(1, count - fixed)
        return jnp.zeros((count,), jnp.int32).at[ranking[jnp.where(places < fixed, places, shifted)]].set(jnp.asarray(sizes, jnp.int32))

    sizes = jnp.where(number % 4 == 0, named(heavy_load, number // 4), named(usual, number - number // 4 - 1))
    mixed = jax.random.permutation(jax.random.fold_in(own, 3), count)
    giver, receiver = mixed[0:count // 2 * 2:2], mixed[1:count // 2 * 2:2]
    margin = jnp.minimum(sizes[giver] - 1, bound - sizes[receiver]) // 2
    margin = jnp.where((giver == ranking[0]) | (receiver == ranking[0]) | (sizes[receiver] == 0), 0, jnp.maximum(margin, 0))
    shifted = jax.random.randint(jax.random.fold_in(own, 4), (count // 2,), 0, 1 << 20) % (margin + 1)
    sizes = sizes.at[giver].add(-shifted).at[receiver].add(shifted)
    items = jnp.searchsorted(jnp.cumsum(sizes), jnp.arange(rows * top), side="right").astype(jnp.int32)
    listing = items.reshape(top, rows).T
    listing = listing[jax.random.permutation(jax.random.fold_in(own, 1), rows)]
    rotation = jax.random.randint(jax.random.fold_in(own, 2), (rows, 1), 0, top)
    return jnp.take_along_axis(listing, (jnp.arange(top)[None, :] + rotation) % top, axis=1)


def shares(count, total, limit, skew, full):
    loads = [(1 << 20) // math.isqrt(standing ** skew) + 1 for standing in range(1, count + 1)]
    largest = limit if full else min(limit, max(-(-total // count), total * loads[0] // sum(loads)))
    least = 1 if total - largest >= count - 1 else 0
    holding, rest = [largest] + [least] * (count - 1), total - largest - least * (count - 1)
    while rest > 0:
        movable = [i for i in range(1, count) if holding[i] < largest] or [i for i in range(1, count) if holding[i] < limit]
        whole, budget = sum([loads[i] for i in movable]), rest
        for i in movable:
            addition = min(limit - holding[i], max(1, budget * loads[i] // whole), rest)
            holding[i] = holding[i] + addition
            rest = rest - addition
    return np.array(holding)


def bell_draw(stream_key, dims, scale, limit, cuts=(), kind=jnp.bfloat16):
    array = jax.random.normal(stream_key, dims, jnp.float32) * scale
    if len(cuts) > 0:
        array = level_of(stream_key, dims, cuts, -0.22, 0.18) * array
    return jnp.clip(array, min=-limit, max=limit).astype(kind)


def setup_inputs(seed: int = 0) -> dict:
    seeds = jax.random.split(jax.random.key(seed), 10)
    queries = draw_queries(jax.random.fold_in(seeds[9], 71), 0)
    cache_keys = draw_cache_keys(jax.random.fold_in(seeds[9], 71), 0)
    cache_values = bell_draw(seeds[2], (ROWS, CONTEXT, KV_WIDTH), 1.0, 6.0, ((1, 16), (2, 8)))
    lengths = draw_lengths(jax.random.fold_in(seeds[9], 71), 0)
    new_keys = bell_draw(seeds[4], (SPAN, KV_WIDTH), 1.0, 6.0, ((0, 16), (1, 8)))
    new_values = bell_draw(seeds[5], (SPAN, KV_WIDTH), 1.0, 6.0, ((0, 16), (1, 8)))
    new_rows = plant(jax.random.randint(seeds[6], (SPAN,), 0, ROWS), jax.random.fold_in(seeds[6], 1), 0, ROWS - 1).astype(jnp.int32)
    owners_keys = jax.random.split(jax.random.fold_in(seeds[7], 1), SPAN // NEW_DEV)
    owners_turns = jax.random.permutation(jax.random.fold_in(seeds[7], 3), SPAN // NEW_DEV)
    owners = jax.vmap(lambda own, number: assign_block(jax.random.fold_in(seeds[7], 2), own, number, NEW_DEV, N_GRP, 1, CAP, 2))(owners_keys, owners_turns).reshape((SPAN, 1))
    out_weight = bell_draw(seeds[8], (D, D), D ** -0.5, 0.0625, ((0, 8), (1, 16)))
    return dict(queries=queries, cache_keys=cache_keys, cache_values=cache_values, lengths=lengths, new_keys=new_keys, new_values=new_values, new_rows=new_rows, owners=owners, out_weight=out_weight)


NEG = -1.0e30


def reference(queries, cache_keys, cache_values, lengths, new_keys, new_values, new_rows, owners, out_weight):
    group_size = HEADS // KV_HEADS
    factor = HEAD_DIM ** -0.5
    query_heads = queries.astype(jnp.float32).reshape(ROWS, KV_HEADS, group_size, HEAD_DIM)
    fresh_keys = new_keys.astype(jnp.float32).reshape(SPAN, KV_HEADS, HEAD_DIM)
    fresh_values = new_values.astype(jnp.float32).reshape(SPAN, KV_HEADS, HEAD_DIM)

    def one_row(items):
        query, keys, values, length, row_index = items
        keys = keys.astype(jnp.float32).reshape(CONTEXT, KV_HEADS, HEAD_DIM)
        values = values.astype(jnp.float32).reshape(CONTEXT, KV_HEADS, HEAD_DIM)
        cached = jnp.einsum("kgd,tkd->kgt", query, keys, precision=lax.Precision.HIGHEST) * factor
        fresh = jnp.einsum("kgd,tkd->kgt", query, fresh_keys, precision=lax.Precision.HIGHEST) * factor
        scores = jnp.concatenate([cached, fresh], axis=-1)
        allowed = jnp.concatenate([jnp.arange(CONTEXT, dtype=jnp.int32) < length, new_rows == row_index])
        scores = jnp.where(allowed[None, None, :], scores, NEG)
        highest = jnp.max(scores, axis=-1, keepdims=True)
        weights = jnp.where(allowed[None, None, :], jnp.exp(scores - highest), 0.0)
        total = jnp.sum(weights, axis=-1)
        every_value = jnp.concatenate([values, fresh_values], axis=0)
        output = jnp.einsum("kgt,tkd->kgd", weights, every_value, precision=lax.Precision.HIGHEST) / total[..., None]
        return output.reshape(D).astype(jnp.bfloat16)

    attended = lax.map(one_row, (query_heads, cache_keys, cache_values, lengths, jnp.arange(ROWS, dtype=jnp.int32)))
    mixed = jnp.dot(attended, out_weight, preferred_element_type=jnp.float32).astype(jnp.bfloat16)

    destination = owners[:, 0]
    onehot = (destination[:, None] == jnp.arange(N_GRP, dtype=jnp.int32)[None, :]).astype(jnp.int32)
    onehot = onehot.reshape(N_GRP, NEW_DEV, N_GRP)
    earlier = jnp.cumsum(onehot, axis=1) - onehot
    rank = jnp.sum(earlier * onehot, axis=-1).reshape(SPAN)
    source_block = jnp.arange(SPAN, dtype=jnp.int32) // NEW_DEV
    slot_index = destination * (N_GRP * CAP) + source_block * CAP + rank
    pool_keys = jnp.zeros((POOL, KV_WIDTH), jnp.bfloat16).at[slot_index].set(new_keys)
    pool_values = jnp.zeros((POOL, KV_WIDTH), jnp.bfloat16).at[slot_index].set(new_values)
    return mixed, jnp.stack([pool_keys, pool_values])
```

```python
import functools
import math

import jax
import jax.numpy as jnp
from jax import lax
from jax.experimental import pallas as pl
from jax.experimental.pallas import tpu as pltpu
from jax.sharding import PartitionSpec as P

MESH = pl.DeviceIdType.MESH
NT = (((1,), (1,)), ((), ()))
NN = (((1,), (0,)), ((), ()))
NEG = -1.0e30
FLOOR = -1.0e20
ROWS = 32
GROUP = 8
HEAD = 128
SEQ = 1024
FRESH = 1024
CAP = 128
BATCH = 4
F32 = jnp.float32
BF16 = jnp.bfloat16


def kernel(
    n,
    m,
    q_hbm, ck_hbm, cv_hbm, len_hbm, nk_hbm, nv_hbm, rows_hbm, own_hbm, w_hbm,
    mixed_ref, pool_ref,
    kb, vb, xb, wb, qin, qf, qb, lens, rowb, ownb,
    stage, sc, sf, pc, pf, acc, accf, stats, rs_out, rs_in, ag, tp_out, tp_in,
    in_sem, k_sem, v_sem, own_sem, big_s, big_r, st_s, st_r, rs_s, rs_r, ag_s, ag_r, tp_s, tp_r,
):
    g = lax.axis_index("grp")
    t = lax.axis_index("tp")
    scale = (HEAD**-0.5) * math.log2(math.e)
    steps = ROWS // BATCH
    chunk = ROWS * GROUP // n

    small = [
        pltpu.make_async_copy(own_hbm, ownb, in_sem.at[0]),
        pltpu.make_async_copy(nk_hbm, xb.at[:, pl.ds(0, HEAD)], in_sem.at[1]),
        pltpu.make_async_copy(nv_hbm, xb.at[:, pl.ds(HEAD, HEAD)], in_sem.at[2]),
        pltpu.make_async_copy(q_hbm, qin, in_sem.at[3]),
        pltpu.make_async_copy(rows_hbm, rowb, in_sem.at[4]),
        pltpu.make_async_copy(len_hbm, lens, in_sem.at[5]),
    ]
    weight = pltpu.make_async_copy(w_hbm, wb, in_sem.at[6])
    keys = [
        pltpu.make_async_copy(ck_hbm.at[pl.ds(c * BATCH, BATCH)], kb.at[pl.ds(c * BATCH, BATCH)], k_sem.at[c])
        for c in range(steps)
    ]
    values = [
        pltpu.make_async_copy(cv_hbm.at[pl.ds(c * BATCH, BATCH)], vb.at[pl.ds(c * BATCH, BATCH)], v_sem.at[c])
        for c in range(steps)
    ]
    for copy in small + keys:
        copy.start()

    barrier = pltpu.get_barrier_semaphore()
    for r in range(1, n):
        pl.semaphore_signal(barrier, inc=1, device_id=(lax.rem(g + r, n), t), device_id_type=MESH)
    for r in range(1, m):
        pl.semaphore_signal(barrier, inc=1, device_id=(g, lax.rem(t + r, m)), device_id_type=MESH)

    small[0].wait()
    own = ownb[...]
    blocks = FRESH // HEAD
    hot = jnp.concatenate([(own == o).astype(F32) for o in range(n)], axis=0).astype(BF16)
    ri = lax.broadcasted_iota(jnp.int32, (HEAD, HEAD), 0)
    ci = lax.broadcasted_iota(jnp.int32, (HEAD, HEAD), 1)
    before = (ri < ci).astype(F32).astype(BF16)
    ra = lax.broadcasted_iota(jnp.int32, (n * blocks, n * blocks), 0)
    ca = lax.broadcasted_iota(jnp.int32, (n * blocks, n * blocks), 1)
    upper = jnp.logical_and(ra // blocks == ca // blocks, ca < ra).astype(F32).astype(BF16)
    within = lax.dot_general(hot, before, NN, preferred_element_type=F32)
    ahead = lax.dot_general(upper, hot, NN, preferred_element_type=F32).astype(BF16)
    ahead = lax.dot_general(ahead, jnp.ones((HEAD, HEAD), BF16), NN, preferred_element_type=F32)
    counted = (within + ahead) * hot.astype(F32)
    rank = counted[0:blocks]
    for o in range(1, n):
        rank = rank + counted[o * blocks : (o + 1) * blocks]

    small[1].wait()
    small[2].wait()
    place = lax.broadcasted_iota(jnp.int32, (CAP, HEAD), 0).astype(F32).astype(BF16)
    big = [None] * n
    per = 4
    for part in range(n // per):
        lhs = []
        for r in range(part * per + 1, part * per + per + 1):
            d = lax.rem(g + r, n)
            named = jnp.where(own == d, rank, -1.0)
            columns = []
            for c in range(blocks):
                line = jnp.broadcast_to(named[c : c + 1, :], (CAP, HEAD)).astype(BF16)
                columns.append(jnp.where(line == place, jnp.bfloat16(1), jnp.bfloat16(0)))
            lhs.append(jnp.concatenate(columns, axis=1))
        placed = lax.dot_general(
            jnp.concatenate(lhs, axis=0), xb[...], NN, preferred_element_type=F32
        ).astype(BF16)
        for i in range(per):
            r = part * per + 1 + i
            stage[r % n, 0] = placed[i * CAP : (i + 1) * CAP, :HEAD]
            stage[r % n, 1] = placed[i * CAP : (i + 1) * CAP, HEAD:]
        if part == 0:
            pl.semaphore_wait(barrier, n - 1 + m - 1)
        for i in range(per):
            r = part * per + 1 + i
            if r < n:
                big[r] = pltpu.make_async_remote_copy(
                    src_ref=stage.at[r],
                    dst_ref=pool_ref.at[:, pl.ds(pl.multiple_of(g * CAP, CAP), CAP), :],
                    send_sem=big_s.at[r],
                    recv_sem=big_r.at[r],
                    device_id=(lax.rem(g + r, n), t),
                    device_id_type=MESH,
                )
                big[r].start()
    mine = pltpu.make_async_copy(
        stage.at[0], pool_ref.at[:, pl.ds(pl.multiple_of(g * CAP, CAP), CAP), :], own_sem
    )
    mine.start()
    for copy in values:
        copy.start()
    weight.start()

    for i in (3, 4, 5):
        small[i].wait()
    for h in range(GROUP):
        qf[pl.ds(h, ROWS, stride=GROUP), :] = qin[:, h * HEAD : (h + 1) * HEAD].astype(F32)
    qb[...] = qf[...].astype(BF16)
    fresh = lax.dot_general(qb[...], xb[:, :HEAD], NT, preferred_element_type=F32)
    seq_of = lax.broadcasted_iota(jnp.int32, (ROWS * GROUP, HEAD), 0) // GROUP
    for c in range(blocks):
        line = jnp.broadcast_to(rowb[c : c + 1, :], (ROWS * GROUP, HEAD))
        sf[:, c * HEAD : (c + 1) * HEAD] = jnp.where(line == seq_of, fresh[:, c * HEAD : (c + 1) * HEAD], NEG)

    pair = 2 * GROUP
    half = lax.broadcasted_iota(jnp.int32, (pair, 2 * HEAD), 0) // GROUP
    side = lax.broadcasted_iota(jnp.int32, (pair, 2 * HEAD), 1) // HEAD
    diagonal = half == side
    position = lax.broadcasted_iota(jnp.int32, (pair, SEQ), 1)
    upper_half = lax.broadcasted_iota(jnp.int32, (pair, SEQ), 0) < GROUP
    lane = lax.broadcasted_iota(jnp.int32, (GROUP, HEAD), 1)

    def score(c):
        for b in range(c * BATCH, (c + 1) * BATCH, 2):
            q = qb[pl.ds(b * GROUP, pair), :]
            q = jnp.where(diagonal, jnp.concatenate([q, q], axis=1), jnp.bfloat16(0))
            k = jnp.concatenate([kb[b], kb[b + 1]], axis=1)
            s = lax.dot_general(q, k, NT, preferred_element_type=F32)
            limit = jnp.where(upper_half, lens[b] - g * SEQ, lens[b + 1] - g * SEQ)
            sc[pl.ds(b * GROUP, pair), :] = jnp.where(position < limit, s, NEG)

    def weigh(c, held):
        for b in range(c * BATCH, (c + 1) * BATCH, 2):
            s = sc[pl.ds(b * GROUP, pair), :]
            f = sf[pl.ds(b * GROUP, pair), :]
            high = jnp.max(jnp.maximum(s, f), axis=1, keepdims=True)
            high = jnp.maximum(high, FLOOR)
            ps = jnp.exp2((s - high) * scale)
            pfr = jnp.exp2((f - high) * scale)
            total = jnp.sum(ps + pfr, axis=1, keepdims=True)
            pc[pl.ds(b * GROUP, pair), :] = ps.astype(BF16)
            pf[pl.ds(b * GROUP, pair), :] = pfr.astype(BF16)
            for j in range(2):
                rows = slice(j * GROUP, (j + 1) * GROUP)
                held = jnp.where(lane == b + j, high[rows], held)
                held = jnp.where(lane == ROWS + b + j, total[rows], held)
        return held

    def add_up(c):
        for b in range(c * BATCH, (c + 1) * BATCH, 2):
            v = jnp.concatenate([vb[b], vb[b + 1]], axis=1)
            o = lax.dot_general(pc[pl.ds(b * GROUP, pair), :], v, NN, preferred_element_type=F32)
            acc[pl.ds(b * GROUP, GROUP), :] = o[:GROUP, :HEAD]
            acc[pl.ds(b * GROUP + GROUP, GROUP), :] = o[GROUP:, HEAD:]

    held = jnp.zeros((GROUP, HEAD), F32)
    for c in range(steps + 1):
        if c < steps:
            keys[c].wait()
            score(c)
        if c >= 1:
            held = weigh(c - 1, held)

    stats[g] = held
    sent = []
    for r in range(1, n):
        copy = pltpu.make_async_remote_copy(
            src_ref=stats.at[g],
            dst_ref=stats.at[g],
            send_sem=st_s.at[r],
            recv_sem=st_r.at[r],
            device_id=(lax.rem(g + r, n), t),
            device_id_type=MESH,
        )
        copy.start()
        sent.append(copy)
    accf[...] = lax.dot_general(pf[...], xb[:, HEAD:], NN, preferred_element_type=F32)
    for c in range(steps):
        values[c].wait()
        add_up(c)

    for copy in sent:
        copy.wait_recv()
    every = [stats[i] for i in range(n)]
    top = functools.reduce(jnp.maximum, every)
    whole = jnp.zeros((GROUP, HEAD), F32)
    for one in every:
        whole = whole + jnp.exp2((one - top) * scale) * pltpu.roll(one, HEAD - ROWS, 1)
    factor = jnp.exp2((held - top) * scale) / whole
    for b in range(ROWS):
        rows = pl.ds(b * GROUP, GROUP)
        acc[rows, :] = (acc[rows, :] + accf[rows, :]) * factor[:, b : b + 1]
    rs_out[...] = acc[...].astype(BF16).reshape(n, chunk, HEAD)
    rs_in[g] = rs_out[g]
    shared = []
    for r in range(1, n):
        d = lax.rem(g + r, n)
        copy = pltpu.make_async_remote_copy(
            src_ref=rs_out.at[d],
            dst_ref=rs_in.at[g],
            send_sem=rs_s.at[r],
            recv_sem=rs_r.at[r],
            device_id=(d, t),
            device_id_type=MESH,
        )
        copy.start()
        shared.append(copy)
    for copy in shared:
        copy.wait_recv()
    attended = rs_in[0].astype(F32)
    for i in range(1, n):
        attended = attended + rs_in[i].astype(F32)
    ag[g] = attended.astype(BF16)
    gathered = []
    for r in range(1, n):
        copy = pltpu.make_async_remote_copy(
            src_ref=ag.at[g],
            dst_ref=ag.at[g],
            send_sem=ag_s.at[r],
            recv_sem=ag_r.at[r],
            device_id=(lax.rem(g + r, n), t),
            device_id_type=MESH,
        )
        copy.start()
        gathered.append(copy)
    weight.wait()
    for copy in gathered:
        copy.wait_recv()

    qf[...] = ag[...].reshape(ROWS * GROUP, HEAD).astype(F32)
    heads = [qf[pl.ds(h, ROWS, stride=GROUP), :].astype(BF16) for h in range(GROUP)]
    term = lax.dot_general(jnp.concatenate(heads, axis=1), wb[...], NN, preferred_element_type=F32)
    low = lax.broadcasted_iota(jnp.int32, (ROWS // 2, HEAD), 1) < HEAD // 2
    for j in range(m // 2):
        first = term[: ROWS // 2, j * HEAD : (j + 1) * HEAD]
        second = term[ROWS // 2 :, j * HEAD : (j + 1) * HEAD]
        tp_out[2 * j] = jnp.where(low, first, pltpu.roll(second, HEAD // 2, 1)).astype(BF16)
        tp_out[2 * j + 1] = jnp.where(low, pltpu.roll(first, HEAD // 2, 1), second).astype(BF16)
    tp_in[t] = tp_out[t]
    terms = []
    for r in range(1, m):
        d = lax.rem(t + r, m)
        copy = pltpu.make_async_remote_copy(
            src_ref=tp_out.at[d],
            dst_ref=tp_in.at[t],
            send_sem=tp_s.at[r],
            recv_sem=tp_r.at[r],
            device_id=(g, d),
            device_id_type=MESH,
        )
        copy.start()
        terms.append(copy)
    for copy in terms:
        copy.wait_recv()
    mixed = tp_in[0].astype(F32)
    for i in range(1, m):
        mixed = mixed + tp_in[i].astype(F32)
    mixed_ref[: ROWS // 2, :] = mixed[:, : HEAD // 2].astype(BF16)
    mixed_ref[ROWS // 2 :, :] = pltpu.roll(mixed, HEAD // 2, 1)[:, : HEAD // 2].astype(BF16)

    for copy in sent + shared + gathered + terms + big[1:]:
        copy.wait_send()
    mine.wait()
    for copy in big[1:]:
        copy.wait_recv()


def on_device(n, m, queries, cache_keys, cache_values, lengths, new_keys, new_values, new_rows, owners, out_weight):
    any_space = pl.BlockSpec(memory_space=pl.ANY)
    dma = pltpu.SemaphoreType.DMA
    steps = ROWS // BATCH
    return pl.pallas_call(
        functools.partial(kernel, n, m),
        out_shape=(
            jax.ShapeDtypeStruct((ROWS, HEAD // 2), BF16),
            jax.ShapeDtypeStruct((2, n * CAP, HEAD), BF16),
        ),
        in_specs=[any_space] * 9,
        out_specs=(pl.BlockSpec(memory_space=pltpu.VMEM), any_space),
        scratch_shapes=[
            pltpu.VMEM((ROWS, SEQ, HEAD), BF16),
            pltpu.VMEM((ROWS, SEQ, HEAD), BF16),
            pltpu.VMEM((FRESH, 2 * HEAD), BF16),
            pltpu.VMEM(out_weight.shape, BF16),
            pltpu.VMEM((ROWS, GROUP * HEAD), BF16),
            pltpu.VMEM((ROWS * GROUP, HEAD), F32),
            pltpu.VMEM((ROWS * GROUP, HEAD), BF16),
            pltpu.SMEM((ROWS,), jnp.int32),
            pltpu.VMEM((FRESH // HEAD, HEAD), jnp.int32),
            pltpu.VMEM((FRESH // HEAD, HEAD), jnp.int32),
            pltpu.VMEM((n, 2, CAP, HEAD), BF16),
            pltpu.VMEM((ROWS * GROUP, SEQ), F32),
            pltpu.VMEM((ROWS * GROUP, FRESH), F32),
            pltpu.VMEM((ROWS * GROUP, SEQ), BF16),
            pltpu.VMEM((ROWS * GROUP, FRESH), BF16),
            pltpu.VMEM((ROWS * GROUP, HEAD), F32),
            pltpu.VMEM((ROWS * GROUP, HEAD), F32),
            pltpu.VMEM((n, GROUP, HEAD), F32),
            pltpu.VMEM((n, ROWS * GROUP // n, HEAD), BF16),
            pltpu.VMEM((n, ROWS * GROUP // n, HEAD), BF16),
            pltpu.VMEM((n, ROWS * GROUP // n, HEAD), BF16),
            pltpu.VMEM((m, ROWS // 2, HEAD), BF16),
            pltpu.VMEM((m, ROWS // 2, HEAD), BF16),
            dma((7,)),
            dma((steps,)),
            dma((steps,)),
            dma,
        ]
        + [dma((n,))] * 8
        + [dma((m,))] * 2,
        compiler_params=pltpu.CompilerParams(
            collective_id=0, has_side_effects=True, vmem_limit_bytes=60 << 20
        ),
        name="decode",
    )(
        queries,
        cache_keys,
        cache_values,
        lengths,
        new_keys,
        new_values,
        new_rows.reshape(FRESH // HEAD, HEAD),
        owners.reshape(FRESH // HEAD, HEAD),
        out_weight,
    )


def solution(mesh):
    placed = (
        P(None, "tp"),
        P(None, "grp", "tp"),
        P(None, "grp", "tp"),
        P(),
        P("grp", "tp"),
        P("grp", "tp"),
        P("grp"),
        P("grp", None),
        P("tp", "grp"),
    )
    return jax.shard_map(
        functools.partial(on_device, mesh.shape["grp"], mesh.shape["tp"]),
        mesh=mesh,
        in_specs=placed,
        out_specs=(P(None, ("grp", "tp")), P(None, "grp", "tp")),
        check_vma=False,
    )
```

```python
import functools
import math

import jax
import jax.numpy as jnp
from jax import lax
from jax.experimental import pallas as pl
from jax.experimental.pallas import tpu as pltpu
from jax.sharding import PartitionSpec as P

MESH = pl.DeviceIdType.MESH
NT = (((1,), (1,)), ((), ()))
NN = (((1,), (0,)), ((), ()))
NEG = -1.0e30
FLOOR = -1.0e20
ROWS = 32
GROUP = 8
HEAD = 128
SEQ = 1024
FRESH = 1024
CAP = 128
BATCH = 4
SIDE = 4
PIECES = 4
AHEAD, GREET, FIRST, MIDDLE, LATE = 2, -1, 5, 10, 13
ORDER = tuple(sorted(((a, b) for a in range(SIDE) for b in range(SIDE)), key=lambda o: (-(2 - abs(2 - o[0])) - (2 - abs(2 - o[1])), o)))
F32 = jnp.float32
BF16 = jnp.bfloat16


def kernel(
    n,
    m,
    q_hbm, ck_hbm, cv_hbm, len_hbm, nk_hbm, nv_hbm, rows_hbm, own_hbm, w_hbm,
    mixed_ref, pool_ref,
    kb, vb, xb, wb, qin, qf, qb, lens, rowb, ownb,
    stage, sc, sf, pc, pf, accf, rs_out, rs_in, ag, core_out, core_in, x_out, x_in,
    in_sem, k_sem, v_sem, own_sem, big_s, big_r, rs_s, rs_r, ag_s, ag_r, x_s, x_r,
):
    g = lax.axis_index("grp")
    t = lax.axis_index("tp")
    y, z = g // SIDE, lax.rem(g, SIDE)
    x, core = t // 2, lax.rem(t, 2)
    mine = lax.rem(z + 2 * y, SIDE)
    scale = (HEAD**-0.5) * math.log2(math.e)
    steps = ROWS // BATCH
    part_rows = ROWS // SIDE
    blocks = FRESH // HEAD

    small = [
        pltpu.make_async_copy(own_hbm, ownb, in_sem.at[0]),
        pltpu.make_async_copy(nk_hbm, xb.at[:, pl.ds(0, HEAD)], in_sem.at[1]),
        pltpu.make_async_copy(nv_hbm, xb.at[:, pl.ds(HEAD, HEAD)], in_sem.at[2]),
        pltpu.make_async_copy(q_hbm, qin, in_sem.at[3]),
        pltpu.make_async_copy(rows_hbm, rowb, in_sem.at[4]),
        pltpu.make_async_copy(len_hbm, lens, in_sem.at[5]),
    ]
    weight = pltpu.make_async_copy(w_hbm, wb, in_sem.at[6])
    keys = [
        pltpu.make_async_copy(ck_hbm.at[pl.ds(c * BATCH, BATCH)], kb.at[pl.ds(c * BATCH, BATCH)], k_sem.at[c])
        for c in range(steps)
    ]
    values = [
        pltpu.make_async_copy(cv_hbm.at[pl.ds(c * BATCH, BATCH)], vb.at[pl.ds(c * BATCH, BATCH)], v_sem.at[c])
        for c in range(steps)
    ]
    for copy in small + keys:
        copy.start()

    barrier = pltpu.get_barrier_semaphore()
    for r in range(1, n):
        pl.semaphore_signal(barrier, inc=1, device_id=(lax.rem(g + r, n), t), device_id_type=MESH)
    pl.semaphore_signal(barrier, inc=1, device_id=(g, 2 * x + 1 - core), device_id_type=MESH)
    for r in range(1, SIDE):
        pl.semaphore_signal(
            barrier, inc=1, device_id=(g, 2 * lax.rem(x + r, SIDE) + core), device_id_type=MESH
        )

    small[0].wait()
    own = ownb[...]
    hot = jnp.concatenate([(own == o).astype(F32) for o in range(n)], axis=0).astype(BF16)
    ri = lax.broadcasted_iota(jnp.int32, (HEAD, HEAD), 0)
    ci = lax.broadcasted_iota(jnp.int32, (HEAD, HEAD), 1)
    before = (ri < ci).astype(F32).astype(BF16)
    ra = lax.broadcasted_iota(jnp.int32, (n * blocks, n * blocks), 0)
    ca = lax.broadcasted_iota(jnp.int32, (n * blocks, n * blocks), 1)
    upper = jnp.logical_and(ra // blocks == ca // blocks, ca < ra).astype(F32).astype(BF16)
    within = lax.dot_general(hot, before, NN, preferred_element_type=F32)
    ahead = lax.dot_general(upper, hot, NN, preferred_element_type=F32).astype(BF16)
    ahead = lax.dot_general(ahead, jnp.ones((HEAD, HEAD), BF16), NN, preferred_element_type=F32)
    counted = (within + ahead) * hot.astype(F32)
    rank = counted[0:blocks]
    for o in range(1, n):
        rank = rank + counted[o * blocks : (o + 1) * blocks]

    slot = lax.broadcasted_iota(jnp.int32, (CAP, HEAD), 0).astype(F32).astype(BF16)

    def toward(r):
        dy, dz = ORDER[r - 1]
        return lax.rem(y + dy, SIDE) * SIDE + lax.rem(z + dz, SIDE)

    big = [
        pltpu.make_async_remote_copy(
            src_ref=stage.at[r],
            dst_ref=pool_ref.at[:, pl.ds(pl.multiple_of(g * CAP, CAP), CAP), :],
            send_sem=big_s.at[r],
            recv_sem=big_r.at[r],
            device_id=(toward(r), t),
            device_id_type=MESH,
        )
        for r in range(1, n)
    ]
    own_part = pltpu.make_async_copy(
        stage.at[0], pool_ref.at[:, pl.ds(pl.multiple_of(g * CAP, CAP), CAP), :], own_sem
    )
    per = 4

    def place(part):
        lhs = []
        for r in range(part * per + 1, part * per + per + 1):
            d = toward(r)
            named = jnp.where(own == d, rank, -1.0)
            columns = []
            for c in range(blocks):
                line = jnp.broadcast_to(named[c : c + 1, :], (CAP, HEAD)).astype(BF16)
                columns.append(jnp.where(line == slot, jnp.bfloat16(1), jnp.bfloat16(0)))
            lhs.append(jnp.concatenate(columns, axis=1))
        placed = lax.dot_general(
            jnp.concatenate(lhs, axis=0), xb[...], NN, preferred_element_type=F32
        ).astype(BF16)
        for i in range(per):
            r = part * per + 1 + i
            stage[r % n, 0] = placed[i * CAP : (i + 1) * CAP, :HEAD]
            stage[r % n, 1] = placed[i * CAP : (i + 1) * CAP, HEAD:]

    def send(first, last):
        for r in range(first, last + 1):
            big[r - 1].start()

    small[1].wait()
    small[2].wait()
    for part in range(AHEAD):
        place(part)
    if GREET < 0:
        pl.semaphore_wait(barrier, n - 1 + SIDE)
        send(1, FIRST)

    for i in (3, 4, 5):
        small[i].wait()
    for h in range(GROUP):
        qf[pl.ds(h, ROWS, stride=GROUP), :] = qin[:, h * HEAD : (h + 1) * HEAD].astype(F32)
    qb[...] = qf[...].astype(BF16)
    fresh = lax.dot_general(qb[...], xb[:, :HEAD], NT, preferred_element_type=F32)
    seq_of = lax.broadcasted_iota(jnp.int32, (ROWS * GROUP, HEAD), 0) // GROUP
    for c in range(blocks):
        line = jnp.broadcast_to(rowb[c : c + 1, :], (ROWS * GROUP, HEAD))
        sf[:, c * HEAD : (c + 1) * HEAD] = jnp.where(line == seq_of, fresh[:, c * HEAD : (c + 1) * HEAD], NEG)

    pair = 2 * GROUP
    half = lax.broadcasted_iota(jnp.int32, (pair, 2 * HEAD), 0) // GROUP
    side = lax.broadcasted_iota(jnp.int32, (pair, 2 * HEAD), 1) // HEAD
    diagonal = half == side
    position = lax.broadcasted_iota(jnp.int32, (pair, SEQ), 1)
    upper_half = lax.broadcasted_iota(jnp.int32, (pair, SEQ), 0) < GROUP
    lane = lax.broadcasted_iota(jnp.int32, (GROUP, HEAD), 1)

    def score(c):
        for b in range(c * BATCH, (c + 1) * BATCH, 2):
            q = qb[pl.ds(b * GROUP, pair), :]
            q = jnp.where(diagonal, jnp.concatenate([q, q], axis=1), jnp.bfloat16(0))
            k = jnp.concatenate([kb[b], kb[b + 1]], axis=1)
            s = lax.dot_general(q, k, NT, preferred_element_type=F32)
            limit = jnp.where(upper_half, lens[b] - g * SEQ, lens[b + 1] - g * SEQ)
            sc[pl.ds(b * GROUP, pair), :] = jnp.where(position < limit, s, NEG)

    def weigh(c, held):
        for b in range(c * BATCH, (c + 1) * BATCH, 2):
            s = sc[pl.ds(b * GROUP, pair), :]
            f = sf[pl.ds(b * GROUP, pair), :]
            high = jnp.max(jnp.maximum(s, f), axis=1, keepdims=True)
            high = jnp.maximum(high, FLOOR).astype(BF16).astype(F32)
            ps = jnp.exp2((s - high) * scale)
            pfr = jnp.exp2((f - high) * scale)
            total = jnp.sum(ps + pfr, axis=1, keepdims=True)
            pc[pl.ds(b * GROUP, pair), :] = ps.astype(BF16)
            pf[pl.ds(b * GROUP, pair), :] = pfr.astype(BF16)
            for j in range(2):
                rows = slice(j * GROUP, (j + 1) * GROUP)
                place_of = (b + j) % part_rows
                held = jnp.where(lane == place_of, high[rows], held)
                held = jnp.where(lane == part_rows + place_of, total[rows], held)
        return held

    def add_up(c):
        for b in range(c * BATCH, (c + 1) * BATCH, 2):
            v = jnp.concatenate([vb[b], vb[b + 1]], axis=1)
            o = lax.dot_general(pc[pl.ds(b * GROUP, pair), :], v, NN, preferred_element_type=F32)
            o = jnp.concatenate([o[:GROUP, :HEAD], o[GROUP:, HEAD:]], axis=0) + accf[pl.ds(b * GROUP, pair), :]
            rs_out[b // part_rows, pl.ds((b % part_rows) * GROUP, pair), :] = o.astype(BF16)

    held = [jnp.zeros((GROUP, HEAD), F32)] * SIDE
    each = part_rows // BATCH
    for c in range(steps + 1):
        if c < steps:
            keys[c].wait()
            values[c].start()
            if c == GREET:
                pl.semaphore_wait(barrier, n - 1 + SIDE)
                send(1, FIRST)
            score(c)
        if c >= 1:
            held[(c - 1) // each] = weigh(c - 1, held[(c - 1) // each])
    for j in range(SIDE):
        coarse = held[j].astype(BF16)
        rest = (held[j] - coarse.astype(F32)).astype(BF16)
        rs_out[j, pl.ds(part_rows * GROUP, pair), :] = jnp.concatenate([coarse, rest], axis=0)
    accf[...] = lax.dot_general(pf[...], xb[:, HEAD:], NN, preferred_element_type=F32)

    weight.start()
    if GREET >= steps:
        pl.semaphore_wait(barrier, n - 1 + SIDE)
        send(1, FIRST)

    for j in range(SIDE):
        for c in range(j * each, (j + 1) * each):
            values[c].wait()
            add_up(c)
        for r in range(SIDE):
            yy = lax.rem(y + r, SIDE)
            d = yy * SIDE + lax.rem(j + 2 * yy, SIDE)
            copy = pltpu.make_async_remote_copy(
                src_ref=rs_out.at[j],
                dst_ref=rs_in.at[g],
                send_sem=rs_s.at[d],
                recv_sem=rs_r.at[g],
                device_id=(d, t),
                device_id_type=MESH,
            )
            if r == 0:
                pl.when(d != g)(copy.start)
            else:
                copy.start()
    for part in range(n // per):
        if part >= AHEAD:
            place(part)
        send(max(FIRST, part * per) + 1, min((part + 1) * per, MIDDLE))
    own_part.start()
    rs_in[g] = rs_out[mine]
    for r in range(1, n):
        i = lax.rem(g + r, n)
        pltpu.make_async_copy(rs_in.at[i], rs_in.at[i], rs_r.at[i]).wait()
    tails = [rs_in[i, pl.ds(part_rows * GROUP, pair), :].astype(F32) for i in range(n)]
    highs = [tail[:GROUP] for tail in tails]
    sums = [pltpu.roll(tail[:GROUP] + tail[GROUP:], HEAD - part_rows, 1) for tail in tails]
    top = functools.reduce(jnp.maximum, highs)
    parts = [jnp.exp2((one - top) * scale) for one in highs]
    whole = parts[0] * sums[0]
    for i in range(1, n):
        whole = whole + parts[i] * sums[i]
    inverse = 1.0 / whole
    parts = [one * inverse for one in parts]
    for b in range(0, part_rows, 2):
        rows = pl.ds(b * GROUP, pair)
        total = jnp.zeros((pair, HEAD), F32)
        for i in range(n):
            factor = jnp.concatenate(
                [jnp.broadcast_to(parts[i][:, b + j : b + j + 1], (GROUP, HEAD)) for j in range(2)], axis=0
            )
            total = total + rs_in[i, rows, :].astype(F32) * factor
        ag[mine, rows, :] = total.astype(BF16)
    gathered = []
    for k, d in enumerate(
        (
            y * SIDE + lax.rem(z + 1, SIDE),
            y * SIDE + lax.rem(z + SIDE - 1, SIDE),
            lax.rem(y + 1, SIDE) * SIDE + z,
        )
    ):
        copy = pltpu.make_async_remote_copy(
            src_ref=ag.at[mine],
            dst_ref=ag.at[mine],
            send_sem=ag_s.at[k],
            recv_sem=ag_r.at[k],
            device_id=(d, t),
            device_id_type=MESH,
        )
        copy.start()
        gathered.append(copy)
    send(MIDDLE + 1, LATE)
    weight.wait()
    for copy in gathered:
        copy.wait_recv()

    qf[...] = ag[...].reshape(ROWS * GROUP, HEAD).astype(F32)
    heads = [qf[pl.ds(h, ROWS, stride=GROUP), :].astype(BF16) for h in range(GROUP)]
    term = lax.dot_general(jnp.concatenate(heads, axis=1), wb[...], NN, preferred_element_type=F32)
    low = lax.broadcasted_iota(jnp.int32, (ROWS // 2, HEAD), 1) < HEAD // 2
    for j in range(SIDE):
        first = term[: ROWS // 2, j * HEAD : (j + 1) * HEAD]
        second = term[ROWS // 2 :, j * HEAD : (j + 1) * HEAD]
        core_out[0, j] = jnp.where(low, first, pltpu.roll(second, HEAD // 2, 1))
        core_out[1, j] = jnp.where(low, pltpu.roll(first, HEAD // 2, 1), second)
    across = pltpu.make_async_remote_copy(
        src_ref=core_out.at[1 - core],
        dst_ref=core_in,
        send_sem=x_s.at[0],
        recv_sem=x_r.at[0],
        device_id=(g, 2 * x + 1 - core),
        device_id_type=MESH,
    )
    across.start()
    across.wait_recv()
    x_out[...] = core_out[core] + core_in[...]
    terms = []
    for r in range(1, SIDE):
        d = lax.rem(x + r, SIDE)
        copy = pltpu.make_async_remote_copy(
            src_ref=x_out.at[d],
            dst_ref=x_in.at[r],
            send_sem=x_s.at[r],
            recv_sem=x_r.at[r],
            device_id=(g, 2 * d + core),
            device_id_type=MESH,
        )
        copy.start()
        terms.append(copy)
    send(LATE + 1, n - 1)
    mixed = x_out[x]
    for r in range(1, SIDE):
        terms[r - 1].wait_recv()
        mixed = mixed + x_in[r]
    mixed_ref[: ROWS // 2, :] = mixed[:, : HEAD // 2].astype(BF16)
    mixed_ref[ROWS // 2 :, :] = pltpu.roll(mixed, HEAD // 2, 1)[:, : HEAD // 2].astype(BF16)

    for r in range(1, n):
        d = lax.rem(g + r, n)
        pltpu.make_async_copy(rs_in.at[d], rs_in.at[d], rs_s.at[d]).wait()
    for copy in gathered + [across] + terms + big:
        copy.wait_send()
    own_part.wait()
    for copy in big:
        copy.wait_recv()


def finish(mixed_in, pool_in, mixed_out, pool_out, sems):
    copies = [
        pltpu.make_async_copy(mixed_in, mixed_out, sems.at[0]),
        pltpu.make_async_copy(pool_in, pool_out, sems.at[1]),
    ]
    for copy in copies:
        copy.start()
    for copy in copies:
        copy.wait()


def on_device(n, m, queries, cache_keys, cache_values, lengths, new_keys, new_values, new_rows, owners, out_weight):
    any_space = pl.BlockSpec(memory_space=pl.ANY)
    vmem_space = pl.BlockSpec(memory_space=pltpu.VMEM)
    dma = pltpu.SemaphoreType.DMA
    steps = ROWS // BATCH
    wide = ROWS * GROUP
    shapes = (
        jax.ShapeDtypeStruct((ROWS, HEAD // 2), BF16),
        jax.ShapeDtypeStruct((2, n * CAP, HEAD), BF16),
    )
    made = pl.pallas_call(
        functools.partial(kernel, n, m),
        out_shape=tuple(pltpu.VMEM(shape.shape, shape.dtype) for shape in shapes),
        in_specs=[any_space] * 9,
        out_specs=(vmem_space, vmem_space),
        scratch_shapes=[
            pltpu.VMEM((ROWS, SEQ, HEAD), BF16),
            pltpu.VMEM((ROWS, SEQ, HEAD), BF16),
            pltpu.VMEM((FRESH, 2 * HEAD), BF16),
            pltpu.VMEM(out_weight.shape, BF16),
            pltpu.VMEM((ROWS, GROUP * HEAD), BF16),
            pltpu.VMEM((wide, HEAD), F32),
            pltpu.VMEM((wide, HEAD), BF16),
            pltpu.SMEM((ROWS,), jnp.int32),
            pltpu.VMEM((FRESH // HEAD, HEAD), jnp.int32),
            pltpu.VMEM((FRESH // HEAD, HEAD), jnp.int32),
            pltpu.VMEM((n, 2, CAP, HEAD), BF16),
            pltpu.VMEM((wide, SEQ), F32),
            pltpu.VMEM((wide, FRESH), F32),
            pltpu.VMEM((wide, SEQ), BF16),
            pltpu.VMEM((wide, FRESH), BF16),
            pltpu.VMEM((wide, HEAD), F32),
            pltpu.VMEM((SIDE, wide // SIDE + 2 * GROUP, HEAD), BF16),
            pltpu.VMEM((n, wide // SIDE + 2 * GROUP, HEAD), BF16),
            pltpu.VMEM((SIDE, wide // SIDE, HEAD), BF16),
            pltpu.VMEM((2, SIDE, ROWS // 2, HEAD), F32),
            pltpu.VMEM((SIDE, ROWS // 2, HEAD), F32),
            pltpu.VMEM((SIDE, ROWS // 2, HEAD), F32),
            pltpu.VMEM((SIDE, ROWS // 2, HEAD), F32),
            dma((7,)),
            dma((steps,)),
            dma((steps,)),
            dma,
        ]
        + [dma((n,))] * 4
        + [dma((SIDE,))] * 4,
        compiler_params=pltpu.CompilerParams(
            collective_id=0, has_side_effects=True, vmem_limit_bytes=60 << 20
        ),
        name="decode",
    )(
        queries,
        cache_keys,
        cache_values,
        lengths,
        new_keys,
        new_values,
        new_rows.reshape(FRESH // HEAD, HEAD),
        owners.reshape(FRESH // HEAD, HEAD),
        out_weight,
    )
    return pl.pallas_call(
        finish,
        out_shape=shapes,
        in_specs=[vmem_space] * 2,
        out_specs=(any_space, any_space),
        scratch_shapes=[dma((2,))],
        compiler_params=pltpu.CompilerParams(vmem_limit_bytes=60 << 20),
        name="finish",
    )(*(pltpu.with_memory_space_constraint(one, pltpu.VMEM) for one in made))


def solution(mesh):
    placed = (
        P(None, "tp"),
        P(None, "grp", "tp"),
        P(None, "grp", "tp"),
        P(),
        P("grp", "tp"),
        P("grp", "tp"),
        P("grp"),
        P("grp", None),
        P("tp", "grp"),
    )
    return jax.shard_map(
        functools.partial(on_device, mesh.shape["grp"], mesh.shape["tp"]),
        mesh=mesh,
        in_specs=placed,
        out_specs=(P(None, ("grp", "tp")), P(None, "grp", "tp")),
        check_vma=False,
    )
```

```python
import functools
import math

import jax
import jax.numpy as jnp
from jax import lax
from jax.experimental import pallas as pl
from jax.experimental.pallas import tpu as pltpu
from jax.sharding import PartitionSpec as P

MESH = pl.DeviceIdType.MESH
NT = (((1,), (1,)), ((), ()))
NN = (((1,), (0,)), ((), ()))
NEG = -1.0e30
FLOOR = -1.0e20
ROWS = 32
GROUP = 8
HEAD = 128
SEQ = 1024
FRESH = 1024
CAP = 128
BATCH = 4
SIDE = 4
PIECES = 4
PLACES = ((1, 6), (7, 10), (11, 13), (14, 16))
AHEAD, GREET, FIRST, MIDDLE, LATE, LAST = 2, -1, 5, 6, 8, 13
ORDER = tuple(sorted(((a, b) for a in range(SIDE) for b in range(SIDE)), key=lambda o: (-(2 - abs(2 - o[0])) - (2 - abs(2 - o[1])), o)))
F32 = jnp.float32
BF16 = jnp.bfloat16


def kernel(
    n,
    m,
    q_hbm, ck_hbm, cv_hbm, len_hbm, nk_hbm, nv_hbm, rows_hbm, own_hbm, w_hbm,
    mixed_ref, pool_ref,
    kb, vb, xb, wb, qin, qf, qb, lens, rowb, ownb,
    stage, sc, sf, pc, pf, accf, rs_out, rs_in, ag, core_out, core_in, x_out, x_in,
    in_sem, k_sem, v_sem, own_sem, big_s, big_r, rs_s, rs_r, ag_s, ag_r, x_s, x_r,
):
    g = lax.axis_index("grp")
    t = lax.axis_index("tp")
    y, z = g // SIDE, lax.rem(g, SIDE)
    x, core = t // 2, lax.rem(t, 2)
    mine = lax.rem(z + 2 * y, SIDE)
    scale = (HEAD**-0.5) * math.log2(math.e)
    steps = ROWS // BATCH
    part_rows = ROWS // SIDE
    blocks = FRESH // HEAD

    small = [
        pltpu.make_async_copy(own_hbm, ownb, in_sem.at[0]),
        pltpu.make_async_copy(nk_hbm, xb.at[:, pl.ds(0, HEAD)], in_sem.at[1]),
        pltpu.make_async_copy(nv_hbm, xb.at[:, pl.ds(HEAD, HEAD)], in_sem.at[2]),
        pltpu.make_async_copy(q_hbm, qin, in_sem.at[3]),
        pltpu.make_async_copy(rows_hbm, rowb, in_sem.at[4]),
        pltpu.make_async_copy(len_hbm, lens, in_sem.at[5]),
    ]
    weight = pltpu.make_async_copy(w_hbm, wb, in_sem.at[6])
    keys = [
        pltpu.make_async_copy(ck_hbm.at[pl.ds(c * BATCH, BATCH)], kb.at[pl.ds(c * BATCH, BATCH)], k_sem.at[c])
        for c in range(steps)
    ]
    values = [
        pltpu.make_async_copy(cv_hbm.at[pl.ds(c * BATCH, BATCH)], vb.at[pl.ds(c * BATCH, BATCH)], v_sem.at[c])
        for c in range(steps)
    ]
    for copy in small + keys:
        copy.start()

    barrier = pltpu.get_barrier_semaphore()
    for r in range(1, n):
        pl.semaphore_signal(barrier, inc=1, device_id=(lax.rem(g + r, n), t), device_id_type=MESH)
    pl.semaphore_signal(barrier, inc=1, device_id=(g, 2 * x + 1 - core), device_id_type=MESH)
    for r in range(1, SIDE):
        pl.semaphore_signal(
            barrier, inc=1, device_id=(g, 2 * lax.rem(x + r, SIDE) + core), device_id_type=MESH
        )

    small[0].wait()
    own = ownb[...]
    hot = jnp.concatenate([(own == o).astype(F32) for o in range(n)], axis=0).astype(BF16)
    ri = lax.broadcasted_iota(jnp.int32, (HEAD, HEAD), 0)
    ci = lax.broadcasted_iota(jnp.int32, (HEAD, HEAD), 1)
    before = (ri < ci).astype(F32).astype(BF16)
    ra = lax.broadcasted_iota(jnp.int32, (n * blocks, n * blocks), 0)
    ca = lax.broadcasted_iota(jnp.int32, (n * blocks, n * blocks), 1)
    upper = jnp.logical_and(ra // blocks == ca // blocks, ca < ra).astype(F32).astype(BF16)
    within = lax.dot_general(hot, before, NN, preferred_element_type=F32)
    ahead = lax.dot_general(upper, hot, NN, preferred_element_type=F32).astype(BF16)
    ahead = lax.dot_general(ahead, jnp.ones((HEAD, HEAD), BF16), NN, preferred_element_type=F32)
    counted = (within + ahead) * hot.astype(F32)
    rank = counted[0:blocks]
    for o in range(1, n):
        rank = rank + counted[o * blocks : (o + 1) * blocks]

    slot = lax.broadcasted_iota(jnp.int32, (CAP, HEAD), 0).astype(F32).astype(BF16)

    def toward(r):
        dy, dz = ORDER[r - 1]
        return lax.rem(y + dy, SIDE) * SIDE + lax.rem(z + dz, SIDE)

    big = [
        pltpu.make_async_remote_copy(
            src_ref=stage.at[r],
            dst_ref=pool_ref.at[:, pl.ds(pl.multiple_of(g * CAP, CAP), CAP), :],
            send_sem=big_s.at[r],
            recv_sem=big_r.at[r],
            device_id=(toward(r), t),
            device_id_type=MESH,
        )
        for r in range(1, n)
    ]
    own_part = pltpu.make_async_copy(
        stage.at[0], pool_ref.at[:, pl.ds(pl.multiple_of(g * CAP, CAP), CAP), :], own_sem
    )
    def place(part):
        first, last = PLACES[part]
        lhs = []
        for r in range(first, last + 1):
            d = toward(r)
            named = jnp.where(own == d, rank, -1.0)
            columns = []
            for c in range(blocks):
                line = jnp.broadcast_to(named[c : c + 1, :], (CAP, HEAD)).astype(BF16)
                columns.append(jnp.where(line == slot, jnp.bfloat16(1), jnp.bfloat16(0)))
            lhs.append(jnp.concatenate(columns, axis=1))
        placed = lax.dot_general(
            jnp.concatenate(lhs, axis=0), xb[...], NN, preferred_element_type=F32
        ).astype(BF16)
        for i, r in enumerate(range(first, last + 1)):
            stage[r % n, 0] = placed[i * CAP : (i + 1) * CAP, :HEAD]
            stage[r % n, 1] = placed[i * CAP : (i + 1) * CAP, HEAD:]

    def send(first, last):
        for r in range(first, last + 1):
            big[r - 1].start()

    small[1].wait()
    small[2].wait()
    place(0)
    if GREET < 0:
        pl.semaphore_wait(barrier, n - 1 + SIDE)
        send(1, FIRST)

    for i in (3, 4, 5):
        small[i].wait()
    for h in range(GROUP):
        qf[pl.ds(h, ROWS, stride=GROUP), :] = qin[:, h * HEAD : (h + 1) * HEAD].astype(F32)
    qb[...] = qf[...].astype(BF16)
    fresh = lax.dot_general(qb[...], xb[:, :HEAD], NT, preferred_element_type=F32)
    seq_of = lax.broadcasted_iota(jnp.int32, (ROWS * GROUP, HEAD), 0) // GROUP
    for c in range(blocks):
        line = jnp.broadcast_to(rowb[c : c + 1, :], (ROWS * GROUP, HEAD))
        sf[:, c * HEAD : (c + 1) * HEAD] = jnp.where(line == seq_of, fresh[:, c * HEAD : (c + 1) * HEAD], NEG)

    pair = 2 * GROUP
    half = lax.broadcasted_iota(jnp.int32, (pair, 2 * HEAD), 0) // GROUP
    side = lax.broadcasted_iota(jnp.int32, (pair, 2 * HEAD), 1) // HEAD
    diagonal = half == side
    position = lax.broadcasted_iota(jnp.int32, (pair, SEQ), 1)
    upper_half = lax.broadcasted_iota(jnp.int32, (pair, SEQ), 0) < GROUP
    lane = lax.broadcasted_iota(jnp.int32, (GROUP, HEAD), 1)

    def score(c):
        for b in range(c * BATCH, (c + 1) * BATCH, 2):
            q = qb[pl.ds(b * GROUP, pair), :]
            q = jnp.where(diagonal, jnp.concatenate([q, q], axis=1), jnp.bfloat16(0))
            k = jnp.concatenate([kb[b], kb[b + 1]], axis=1)
            s = lax.dot_general(q, k, NT, preferred_element_type=F32)
            limit = jnp.where(upper_half, lens[b] - g * SEQ, lens[b + 1] - g * SEQ)
            sc[pl.ds(b * GROUP, pair), :] = jnp.where(position < limit, s, NEG)

    def weigh(c, held):
        for b in range(c * BATCH, (c + 1) * BATCH, 2):
            s = sc[pl.ds(b * GROUP, pair), :]
            f = sf[pl.ds(b * GROUP, pair), :]
            high = jnp.max(jnp.maximum(s, f), axis=1, keepdims=True)
            high = jnp.maximum(high, FLOOR).astype(BF16).astype(F32)
            ps = jnp.exp2((s - high) * scale)
            pfr = jnp.exp2((f - high) * scale)
            total = jnp.sum(ps + pfr, axis=1, keepdims=True)
            pc[pl.ds(b * GROUP, pair), :] = ps.astype(BF16)
            pf[pl.ds(b * GROUP, pair), :] = pfr.astype(BF16)
            for j in range(2):
                rows = slice(j * GROUP, (j + 1) * GROUP)
                place_of = (b + j) % part_rows
                held = jnp.where(lane == place_of, high[rows], held)
                held = jnp.where(lane == part_rows + place_of, total[rows], held)
        return held

    def add_up(c):
        for b in range(c * BATCH, (c + 1) * BATCH, 2):
            v = jnp.concatenate([vb[b], vb[b + 1]], axis=1)
            o = lax.dot_general(pc[pl.ds(b * GROUP, pair), :], v, NN, preferred_element_type=F32)
            o = jnp.concatenate([o[:GROUP, :HEAD], o[GROUP:, HEAD:]], axis=0) + accf[pl.ds(b * GROUP, pair), :]
            rs_out[b // part_rows, pl.ds((b % part_rows) * GROUP, pair), :] = o.astype(BF16)

    held = [jnp.zeros((GROUP, HEAD), F32)] * SIDE
    each = part_rows // BATCH
    for c in range(steps + 1):
        if c < steps:
            keys[c].wait()
            values[c].start()
            if c == GREET:
                pl.semaphore_wait(barrier, n - 1 + SIDE)
                send(1, FIRST)
            score(c)
        if c >= 1:
            held[(c - 1) // each] = weigh(c - 1, held[(c - 1) // each])
    for j in range(SIDE):
        coarse = held[j].astype(BF16)
        rest = (held[j] - coarse.astype(F32)).astype(BF16)
        rs_out[j, pl.ds(part_rows * GROUP, pair), :] = jnp.concatenate([coarse, rest], axis=0)
    accf[...] = lax.dot_general(pf[...], xb[:, HEAD:], NN, preferred_element_type=F32)

    weight.start()
    if GREET >= steps:
        pl.semaphore_wait(barrier, n - 1 + SIDE)
        send(1, FIRST)

    for j in range(SIDE):
        for c in range(j * each, (j + 1) * each):
            values[c].wait()
            add_up(c)
        for r in range(SIDE):
            yy = lax.rem(y + r, SIDE)
            d = yy * SIDE + lax.rem(j + 2 * yy, SIDE)
            copy = pltpu.make_async_remote_copy(
                src_ref=rs_out.at[j],
                dst_ref=rs_in.at[g],
                send_sem=rs_s.at[d],
                recv_sem=rs_r.at[g],
                device_id=(d, t),
                device_id_type=MESH,
            )
            if r == 0:
                pl.when(d != g)(copy.start)
            else:
                copy.start()
    send(FIRST + 1, MIDDLE)
    for part in range(1, len(PLACES)):
        place(part)
    own_part.start()
    rs_in[g] = rs_out[mine]
    for r in range(1, n):
        i = lax.rem(g + r, n)
        pltpu.make_async_copy(rs_in.at[i], rs_in.at[i], rs_r.at[i]).wait()
    tails = [rs_in[i, pl.ds(part_rows * GROUP, pair), :].astype(F32) for i in range(n)]
    highs = [tail[:GROUP] for tail in tails]
    sums = [pltpu.roll(tail[:GROUP] + tail[GROUP:], HEAD - part_rows, 1) for tail in tails]
    top = functools.reduce(jnp.maximum, highs)
    parts = [jnp.exp2((one - top) * scale) for one in highs]
    whole = parts[0] * sums[0]
    for i in range(1, n):
        whole = whole + parts[i] * sums[i]
    inverse = 1.0 / whole
    parts = [one * inverse for one in parts]
    for b in range(0, part_rows, 2):
        rows = pl.ds(b * GROUP, pair)
        total = jnp.zeros((pair, HEAD), F32)
        for i in range(n):
            factor = jnp.concatenate(
                [jnp.broadcast_to(parts[i][:, b + j : b + j + 1], (GROUP, HEAD)) for j in range(2)], axis=0
            )
            total = total + rs_in[i, rows, :].astype(F32) * factor
        ag[mine, rows, :] = total.astype(BF16)
    gathered = []
    for k, d in enumerate(
        (
            y * SIDE + lax.rem(z + 1, SIDE),
            y * SIDE + lax.rem(z + SIDE - 1, SIDE),
            lax.rem(y + 1, SIDE) * SIDE + z,
        )
    ):
        copy = pltpu.make_async_remote_copy(
            src_ref=ag.at[mine],
            dst_ref=ag.at[mine],
            send_sem=ag_s.at[k],
            recv_sem=ag_r.at[k],
            device_id=(d, t),
            device_id_type=MESH,
        )
        copy.start()
        gathered.append(copy)
    send(MIDDLE + 1, LATE)
    weight.wait()
    for copy in gathered:
        copy.wait_recv()

    send(LATE + 1, LAST)

    qf[...] = ag[...].reshape(ROWS * GROUP, HEAD).astype(F32)
    heads = [qf[pl.ds(h, ROWS, stride=GROUP), :].astype(BF16) for h in range(GROUP)]
    term = lax.dot_general(jnp.concatenate(heads, axis=1), wb[...], NN, preferred_element_type=F32)
    low = lax.broadcasted_iota(jnp.int32, (ROWS // 2, HEAD), 1) < HEAD // 2
    for j in range(SIDE):
        first = term[: ROWS // 2, j * HEAD : (j + 1) * HEAD]
        second = term[ROWS // 2 :, j * HEAD : (j + 1) * HEAD]
        core_out[0, j] = jnp.where(low, first, pltpu.roll(second, HEAD // 2, 1))
        core_out[1, j] = jnp.where(low, pltpu.roll(first, HEAD // 2, 1), second)
    across = pltpu.make_async_remote_copy(
        src_ref=core_out.at[1 - core],
        dst_ref=core_in,
        send_sem=x_s.at[0],
        recv_sem=x_r.at[0],
        device_id=(g, 2 * x + 1 - core),
        device_id_type=MESH,
    )
    across.start()
    across.wait_recv()
    x_out[...] = core_out[core] + core_in[...]
    terms = []
    for r in range(1, SIDE):
        d = lax.rem(x + r, SIDE)
        copy = pltpu.make_async_remote_copy(
            src_ref=x_out.at[d],
            dst_ref=x_in.at[r],
            send_sem=x_s.at[r],
            recv_sem=x_r.at[r],
            device_id=(g, 2 * d + core),
            device_id_type=MESH,
        )
        copy.start()
        terms.append(copy)
    send(LAST + 1, n - 1)
    mixed = x_out[x]
    for r in range(1, SIDE):
        terms[r - 1].wait_recv()
        mixed = mixed + x_in[r]
    mixed_ref[: ROWS // 2, :] = mixed[:, : HEAD // 2].astype(BF16)
    mixed_ref[ROWS // 2 :, :] = pltpu.roll(mixed, HEAD // 2, 1)[:, : HEAD // 2].astype(BF16)

    for r in range(1, n):
        d = lax.rem(g + r, n)
        pltpu.make_async_copy(rs_in.at[d], rs_in.at[d], rs_s.at[d]).wait()
    for copy in gathered + [across] + terms + big:
        copy.wait_send()
    own_part.wait()
    for copy in big:
        copy.wait_recv()


def finish(mixed_in, pool_in, mixed_out, pool_out, sems):
    copies = [
        pltpu.make_async_copy(mixed_in, mixed_out, sems.at[0]),
        pltpu.make_async_copy(pool_in, pool_out, sems.at[1]),
    ]
    for copy in copies:
        copy.start()
    for copy in copies:
        copy.wait()


def on_device(n, m, queries, cache_keys, cache_values, lengths, new_keys, new_values, new_rows, owners, out_weight):
    any_space = pl.BlockSpec(memory_space=pl.ANY)
    vmem_space = pl.BlockSpec(memory_space=pltpu.VMEM)
    dma = pltpu.SemaphoreType.DMA
    steps = ROWS // BATCH
    wide = ROWS * GROUP
    shapes = (
        jax.ShapeDtypeStruct((ROWS, HEAD // 2), BF16),
        jax.ShapeDtypeStruct((2, n * CAP, HEAD), BF16),
    )
    made = pl.pallas_call(
        functools.partial(kernel, n, m),
        out_shape=tuple(pltpu.VMEM(shape.shape, shape.dtype) for shape in shapes),
        in_specs=[any_space] * 9,
        out_specs=(vmem_space, vmem_space),
        scratch_shapes=[
            pltpu.VMEM((ROWS, SEQ, HEAD), BF16),
            pltpu.VMEM((ROWS, SEQ, HEAD), BF16),
            pltpu.VMEM((FRESH, 2 * HEAD), BF16),
            pltpu.VMEM(out_weight.shape, BF16),
            pltpu.VMEM((ROWS, GROUP * HEAD), BF16),
            pltpu.VMEM((wide, HEAD), F32),
            pltpu.VMEM((wide, HEAD), BF16),
            pltpu.SMEM((ROWS,), jnp.int32),
            pltpu.VMEM((FRESH // HEAD, HEAD), jnp.int32),
            pltpu.VMEM((FRESH // HEAD, HEAD), jnp.int32),
            pltpu.VMEM((n, 2, CAP, HEAD), BF16),
            pltpu.VMEM((wide, SEQ), F32),
            pltpu.VMEM((wide, FRESH), F32),
            pltpu.VMEM((wide, SEQ), BF16),
            pltpu.VMEM((wide, FRESH), BF16),
            pltpu.VMEM((wide, HEAD), F32),
            pltpu.VMEM((SIDE, wide // SIDE + 2 * GROUP, HEAD), BF16),
            pltpu.VMEM((n, wide // SIDE + 2 * GROUP, HEAD), BF16),
            pltpu.VMEM((SIDE, wide // SIDE, HEAD), BF16),
            pltpu.VMEM((2, SIDE, ROWS // 2, HEAD), F32),
            pltpu.VMEM((SIDE, ROWS // 2, HEAD), F32),
            pltpu.VMEM((SIDE, ROWS // 2, HEAD), F32),
            pltpu.VMEM((SIDE, ROWS // 2, HEAD), F32),
            dma((7,)),
            dma((steps,)),
            dma((steps,)),
            dma,
        ]
        + [dma((n,))] * 4
        + [dma((SIDE,))] * 4,
        compiler_params=pltpu.CompilerParams(
            collective_id=0, has_side_effects=True, vmem_limit_bytes=60 << 20
        ),
        name="decode",
    )(
        queries,
        cache_keys,
        cache_values,
        lengths,
        new_keys,
        new_values,
        new_rows.reshape(FRESH // HEAD, HEAD),
        owners.reshape(FRESH // HEAD, HEAD),
        out_weight,
    )
    return pl.pallas_call(
        finish,
        out_shape=shapes,
        in_specs=[vmem_space] * 2,
        out_specs=(any_space, any_space),
        scratch_shapes=[dma((2,))],
        compiler_params=pltpu.CompilerParams(vmem_limit_bytes=60 << 20),
        name="finish",
    )(*(pltpu.with_memory_space_constraint(one, pltpu.VMEM) for one in made))


def solution(mesh):
    placed = (
        P(None, "tp"),
        P(None, "grp", "tp"),
        P(None, "grp", "tp"),
        P(),
        P("grp", "tp"),
        P("grp", "tp"),
        P("grp"),
        P("grp", None),
        P("tp", "grp"),
    )
    return jax.shard_map(
        functools.partial(on_device, mesh.shape["grp"], mesh.shape["tp"]),
        mesh=mesh,
        in_specs=placed,
        out_specs=(P(None, ("grp", "tp")), P(None, "grp", "tp")),
        check_vma=False,
    )
```

```python
import functools
import math

import jax
import jax.numpy as jnp
from jax import lax
from jax.experimental import pallas as pl
from jax.experimental.pallas import tpu as pltpu
from jax.sharding import PartitionSpec as P

MESH = pl.DeviceIdType.MESH
NT = (((1,), (1,)), ((), ()))
NN = (((1,), (0,)), ((), ()))
NEG = -1.0e30
FLOOR = -1.0e20
ROWS = 32
GROUP = 8
HEAD = 128
SEQ = 1024
FRESH = 1024
CAP = 128
BATCH = 4
SIDE = 4
PIECES = 4
PLACES = ((1, 6), (7, 10), (11, 13), (14, 16))
FIRST, MIDDLE, LATE, LAST = 4, 4, 5, 13
ORDER = tuple(sorted(((a, b) for a in range(SIDE) for b in range(SIDE)), key=lambda o: (-(2 - abs(2 - o[0])) - (2 - abs(2 - o[1])), o)))
F32 = jnp.float32
BF16 = jnp.bfloat16


def kernel(
    n,
    m,
    q_hbm, ck_hbm, cv_hbm, len_hbm, nk_hbm, nv_hbm, rows_hbm, own_hbm, w_hbm,
    mixed_ref, pool_ref,
    kb, vb, xb, wb, qin, qf, qb, lens, rowb, ownb,
    stage, sc, sf, pc, pf, accf, rs_out, rs_in, ag, core_out, core_in, x_out, x_in,
    in_sem, k_sem, v_sem, own_sem, big_s, big_r, rs_s, rs_r, ag_s, ag_r, x_s, x_r,
):
    g = lax.axis_index("grp")
    t = lax.axis_index("tp")
    y, z = g // SIDE, lax.rem(g, SIDE)
    x, core = t // 2, lax.rem(t, 2)
    mine = lax.rem(z + 2 * y, SIDE)
    scale = (HEAD**-0.5) * math.log2(math.e)
    steps = ROWS // BATCH
    part_rows = ROWS // SIDE
    blocks = FRESH // HEAD

    small = [
        pltpu.make_async_copy(own_hbm, ownb, in_sem.at[0]),
        pltpu.make_async_copy(nk_hbm, xb.at[:, pl.ds(0, HEAD)], in_sem.at[1]),
        pltpu.make_async_copy(nv_hbm, xb.at[:, pl.ds(HEAD, HEAD)], in_sem.at[2]),
        pltpu.make_async_copy(q_hbm, qin, in_sem.at[3]),
        pltpu.make_async_copy(rows_hbm, rowb, in_sem.at[4]),
        pltpu.make_async_copy(len_hbm, lens, in_sem.at[5]),
    ]
    weight = pltpu.make_async_copy(w_hbm, wb, in_sem.at[6])
    keys = [
        pltpu.make_async_copy(ck_hbm.at[pl.ds(c * BATCH, BATCH)], kb.at[pl.ds(c * BATCH, BATCH)], k_sem.at[c])
        for c in range(steps)
    ]
    values = [
        pltpu.make_async_copy(cv_hbm.at[pl.ds(c * BATCH, BATCH)], vb.at[pl.ds(c * BATCH, BATCH)], v_sem.at[c])
        for c in range(steps)
    ]
    for copy in small + keys:
        copy.start()

    barrier = pltpu.get_barrier_semaphore()
    for r in range(1, n):
        pl.semaphore_signal(barrier, inc=1, device_id=(lax.rem(g + r, n), t), device_id_type=MESH)
    pl.semaphore_signal(barrier, inc=1, device_id=(g, 2 * x + 1 - core), device_id_type=MESH)
    for r in range(1, SIDE):
        pl.semaphore_signal(
            barrier, inc=1, device_id=(g, 2 * lax.rem(x + r, SIDE) + core), device_id_type=MESH
        )

    small[0].wait()
    own = ownb[...]
    hot = jnp.concatenate([(own == o).astype(F32) for o in range(n)], axis=0).astype(BF16)
    ri = lax.broadcasted_iota(jnp.int32, (HEAD, HEAD), 0)
    ci = lax.broadcasted_iota(jnp.int32, (HEAD, HEAD), 1)
    before = (ri < ci).astype(F32).astype(BF16)
    ra = lax.broadcasted_iota(jnp.int32, (n * blocks, n * blocks), 0)
    ca = lax.broadcasted_iota(jnp.int32, (n * blocks, n * blocks), 1)
    upper = jnp.logical_and(ra // blocks == ca // blocks, ca < ra).astype(F32).astype(BF16)
    within = lax.dot_general(hot, before, NN, preferred_element_type=F32)
    ahead = lax.dot_general(upper, hot, NN, preferred_element_type=F32).astype(BF16)
    ahead = lax.dot_general(ahead, jnp.ones((HEAD, HEAD), BF16), NN, preferred_element_type=F32)
    counted = (within + ahead) * hot.astype(F32)
    rank = counted[0:blocks]
    for o in range(1, n):
        rank = rank + counted[o * blocks : (o + 1) * blocks]

    slot = lax.broadcasted_iota(jnp.int32, (CAP, HEAD), 0).astype(F32).astype(BF16)

    def toward(r):
        dy, dz = ORDER[r - 1]
        return lax.rem(y + dy, SIDE) * SIDE + lax.rem(z + dz, SIDE)

    big = [
        pltpu.make_async_remote_copy(
            src_ref=stage.at[r],
            dst_ref=pool_ref.at[:, pl.ds(pl.multiple_of(g * CAP, CAP), CAP), :],
            send_sem=big_s.at[r],
            recv_sem=big_r.at[r],
            device_id=(toward(r), t),
            device_id_type=MESH,
        )
        for r in range(1, n)
    ]
    own_part = pltpu.make_async_copy(
        stage.at[0], pool_ref.at[:, pl.ds(pl.multiple_of(g * CAP, CAP), CAP), :], own_sem
    )
    def place(part):
        first, last = PLACES[part]
        lhs = []
        for r in range(first, last + 1):
            d = toward(r)
            named = jnp.where(own == d, rank, -1.0)
            columns = []
            for c in range(blocks):
                line = jnp.broadcast_to(named[c : c + 1, :], (CAP, HEAD)).astype(BF16)
                columns.append(jnp.where(line == slot, jnp.bfloat16(1), jnp.bfloat16(0)))
            lhs.append(jnp.concatenate(columns, axis=1))
        placed = lax.dot_general(
            jnp.concatenate(lhs, axis=0), xb[...], NN, preferred_element_type=F32
        ).astype(BF16)
        for i, r in enumerate(range(first, last + 1)):
            stage[r % n, 0] = placed[i * CAP : (i + 1) * CAP, :HEAD]
            stage[r % n, 1] = placed[i * CAP : (i + 1) * CAP, HEAD:]

    def send(first, last):
        for r in range(first, last + 1):
            big[r - 1].start()

    small[1].wait()
    small[2].wait()
    place(0)
    pl.semaphore_wait(barrier, n - 1 + SIDE)
    send(1, FIRST)

    for i in (3, 4, 5):
        small[i].wait()
    for h in range(GROUP):
        qf[pl.ds(h, ROWS, stride=GROUP), :] = qin[:, h * HEAD : (h + 1) * HEAD].astype(F32)
    qb[...] = qf[...].astype(BF16)
    fresh = lax.dot_general(qb[...], xb[:, :HEAD], NT, preferred_element_type=F32)
    seq_of = lax.broadcasted_iota(jnp.int32, (ROWS * GROUP, HEAD), 0) // GROUP
    for c in range(blocks):
        line = jnp.broadcast_to(rowb[c : c + 1, :], (ROWS * GROUP, HEAD))
        sf[:, c * HEAD : (c + 1) * HEAD] = jnp.where(line == seq_of, fresh[:, c * HEAD : (c + 1) * HEAD], NEG)

    pair = 2 * GROUP
    half = lax.broadcasted_iota(jnp.int32, (pair, 2 * HEAD), 0) // GROUP
    side = lax.broadcasted_iota(jnp.int32, (pair, 2 * HEAD), 1) // HEAD
    diagonal = half == side
    position = lax.broadcasted_iota(jnp.int32, (pair, SEQ), 1)
    upper_half = lax.broadcasted_iota(jnp.int32, (pair, SEQ), 0) < GROUP
    lane = lax.broadcasted_iota(jnp.int32, (GROUP, HEAD), 1)

    def score(c):
        for b in range(c * BATCH, (c + 1) * BATCH, 2):
            q = qb[pl.ds(b * GROUP, pair), :]
            q = jnp.where(diagonal, jnp.concatenate([q, q], axis=1), jnp.bfloat16(0))
            k = jnp.concatenate([kb[b], kb[b + 1]], axis=1)
            s = lax.dot_general(q, k, NT, preferred_element_type=F32)
            limit = jnp.where(upper_half, lens[b] - g * SEQ, lens[b + 1] - g * SEQ)
            sc[pl.ds(b * GROUP, pair), :] = jnp.where(position < limit, s, NEG)

    def weigh(c, held):
        for b in range(c * BATCH, (c + 1) * BATCH, 2):
            s = sc[pl.ds(b * GROUP, pair), :]
            f = sf[pl.ds(b * GROUP, pair), :]
            high = jnp.max(jnp.maximum(s, f), axis=1, keepdims=True)
            high = jnp.maximum(high, FLOOR).astype(BF16).astype(F32)
            ps = jnp.exp2((s - high) * scale)
            pfr = jnp.exp2((f - high) * scale)
            total = jnp.sum(ps + pfr, axis=1, keepdims=True)
            pc[pl.ds(b * GROUP, pair), :] = ps.astype(BF16)
            pf[pl.ds(b * GROUP, pair), :] = pfr.astype(BF16)
            for j in range(2):
                rows = slice(j * GROUP, (j + 1) * GROUP)
                place_of = (b + j) % part_rows
                held = jnp.where(lane == place_of, high[rows], held)
                held = jnp.where(lane == part_rows + place_of, total[rows], held)
        return held

    def add_up(c):
        for b in range(c * BATCH, (c + 1) * BATCH, 2):
            v = jnp.concatenate([vb[b], vb[b + 1]], axis=1)
            o = lax.dot_general(pc[pl.ds(b * GROUP, pair), :], v, NN, preferred_element_type=F32)
            o = jnp.concatenate([o[:GROUP, :HEAD], o[GROUP:, HEAD:]], axis=0) + accf[pl.ds(b * GROUP, pair), :]
            rs_out[b // part_rows, pl.ds((b % part_rows) * GROUP, pair), :] = o.astype(BF16)

    held = [jnp.zeros((GROUP, HEAD), F32)] * SIDE
    each = part_rows // BATCH
    for c in range(steps + 1):
        if c < steps:
            keys[c].wait()
            values[c].start()
            score(c)
        if c >= 1:
            held[(c - 1) // each] = weigh(c - 1, held[(c - 1) // each])
    for j in range(SIDE):
        coarse = held[j].astype(BF16)
        rest = (held[j] - coarse.astype(F32)).astype(BF16)
        rs_out[j, pl.ds(part_rows * GROUP, pair), :] = jnp.concatenate([coarse, rest], axis=0)
    accf[...] = lax.dot_general(pf[...], xb[:, HEAD:], NN, preferred_element_type=F32)

    weight.start()
    for j in range(SIDE):
        for c in range(j * each, (j + 1) * each):
            values[c].wait()
            add_up(c)
        for r in range(SIDE):
            yy = lax.rem(y + r, SIDE)
            d = yy * SIDE + lax.rem(j + 2 * yy, SIDE)
            copy = pltpu.make_async_remote_copy(
                src_ref=rs_out.at[j],
                dst_ref=rs_in.at[g],
                send_sem=rs_s.at[d],
                recv_sem=rs_r.at[g],
                device_id=(d, t),
                device_id_type=MESH,
            )
            if r == 0:
                pl.when(d != g)(copy.start)
            else:
                copy.start()
    send(FIRST + 1, MIDDLE)
    for part in range(1, len(PLACES)):
        place(part)
    own_part.start()
    rs_in[g] = rs_out[mine]
    for r in range(1, n):
        i = lax.rem(g + r, n)
        pltpu.make_async_copy(rs_in.at[i], rs_in.at[i], rs_r.at[i]).wait()
    tails = [rs_in[i, pl.ds(part_rows * GROUP, pair), :].astype(F32) for i in range(n)]
    highs = [tail[:GROUP] for tail in tails]
    sums = [pltpu.roll(tail[:GROUP] + tail[GROUP:], HEAD - part_rows, 1) for tail in tails]
    top = functools.reduce(jnp.maximum, highs)
    parts = [jnp.exp2((one - top) * scale) for one in highs]
    whole = parts[0] * sums[0]
    for i in range(1, n):
        whole = whole + parts[i] * sums[i]
    inverse = 1.0 / whole
    parts = [one * inverse for one in parts]
    for b in range(0, part_rows, 2):
        rows = pl.ds(b * GROUP, pair)
        total = jnp.zeros((pair, HEAD), F32)
        for i in range(n):
            factor = jnp.concatenate(
                [jnp.broadcast_to(parts[i][:, b + j : b + j + 1], (GROUP, HEAD)) for j in range(2)], axis=0
            )
            total = total + rs_in[i, rows, :].astype(F32) * factor
        ag[mine, rows, :] = total.astype(BF16)
    gathered = []
    for k, d in enumerate(
        (
            lax.rem(y + 1, SIDE) * SIDE + z,
            y * SIDE + lax.rem(z + 1, SIDE),
            y * SIDE + lax.rem(z + SIDE - 1, SIDE),
        )
    ):
        copy = pltpu.make_async_remote_copy(
            src_ref=ag.at[mine],
            dst_ref=ag.at[mine],
            send_sem=ag_s.at[k],
            recv_sem=ag_r.at[k],
            device_id=(d, t),
            device_id_type=MESH,
        )
        copy.start()
        gathered.append(copy)
    send(MIDDLE + 1, LATE)
    weight.wait()
    for copy in gathered:
        copy.wait_recv()

    for r in range(LATE + 1, n):
        pl.when(toward(r) == 0)(big[r - 1].start)
    for r in range(LATE + 1, LAST + 1):
        pl.when(toward(r) != 0)(big[r - 1].start)

    qf[...] = ag[...].reshape(ROWS * GROUP, HEAD).astype(F32)
    heads = [qf[pl.ds(h, ROWS, stride=GROUP), :].astype(BF16) for h in range(GROUP)]
    term = lax.dot_general(jnp.concatenate(heads, axis=1), wb[...], NN, preferred_element_type=F32)
    low = lax.broadcasted_iota(jnp.int32, (ROWS // 2, HEAD), 1) < HEAD // 2
    for j in range(SIDE):
        first = term[: ROWS // 2, j * HEAD : (j + 1) * HEAD]
        second = term[ROWS // 2 :, j * HEAD : (j + 1) * HEAD]
        core_out[0, j] = jnp.where(low, first, pltpu.roll(second, HEAD // 2, 1))
        core_out[1, j] = jnp.where(low, pltpu.roll(first, HEAD // 2, 1), second)
    across = pltpu.make_async_remote_copy(
        src_ref=core_out.at[1 - core],
        dst_ref=core_in,
        send_sem=x_s.at[0],
        recv_sem=x_r.at[0],
        device_id=(g, 2 * x + 1 - core),
        device_id_type=MESH,
    )
    across.start()
    across.wait_recv()
    x_out[...] = core_out[core] + core_in[...]
    terms = []
    for r in (2, 3, 1):
        d = lax.rem(x + r, SIDE)
        copy = pltpu.make_async_remote_copy(
            src_ref=x_out.at[d],
            dst_ref=x_in.at[r],
            send_sem=x_s.at[r],
            recv_sem=x_r.at[r],
            device_id=(g, 2 * d + core),
            device_id_type=MESH,
        )
        copy.start()
        terms.append(copy)
    for r in range(LAST + 1, n):
        pl.when(toward(r) != 0)(big[r - 1].start)
    mixed = x_out[x]
    for r in range(1, SIDE):
        terms[(2, 3, 1).index(r)].wait_recv()
        mixed = mixed + x_in[r]
    mixed_ref[: ROWS // 2, :] = mixed[:, : HEAD // 2].astype(BF16)
    mixed_ref[ROWS // 2 :, :] = pltpu.roll(mixed, HEAD // 2, 1)[:, : HEAD // 2].astype(BF16)

    for r in range(1, n):
        d = lax.rem(g + r, n)
        pltpu.make_async_copy(rs_in.at[d], rs_in.at[d], rs_s.at[d]).wait()
    for copy in gathered + [across] + terms + big:
        copy.wait_send()
    own_part.wait()
    for copy in big:
        copy.wait_recv()


def finish(mixed_in, pool_in, mixed_out, pool_out, sems):
    copies = [
        pltpu.make_async_copy(mixed_in, mixed_out, sems.at[0]),
        pltpu.make_async_copy(pool_in, pool_out, sems.at[1]),
    ]
    for copy in copies:
        copy.start()
    for copy in copies:
        copy.wait()


def on_device(n, m, queries, cache_keys, cache_values, lengths, new_keys, new_values, new_rows, owners, out_weight):
    any_space = pl.BlockSpec(memory_space=pl.ANY)
    vmem_space = pl.BlockSpec(memory_space=pltpu.VMEM)
    dma = pltpu.SemaphoreType.DMA
    steps = ROWS // BATCH
    wide = ROWS * GROUP
    shapes = (
        jax.ShapeDtypeStruct((ROWS, HEAD // 2), BF16),
        jax.ShapeDtypeStruct((2, n * CAP, HEAD), BF16),
    )
    made = pl.pallas_call(
        functools.partial(kernel, n, m),
        out_shape=tuple(pltpu.VMEM(shape.shape, shape.dtype) for shape in shapes),
        in_specs=[any_space] * 9,
        out_specs=(vmem_space, vmem_space),
        scratch_shapes=[
            pltpu.VMEM((ROWS, SEQ, HEAD), BF16),
            pltpu.VMEM((ROWS, SEQ, HEAD), BF16),
            pltpu.VMEM((FRESH, 2 * HEAD), BF16),
            pltpu.VMEM(out_weight.shape, BF16),
            pltpu.VMEM((ROWS, GROUP * HEAD), BF16),
            pltpu.VMEM((wide, HEAD), F32),
            pltpu.VMEM((wide, HEAD), BF16),
            pltpu.SMEM((ROWS,), jnp.int32),
            pltpu.VMEM((FRESH // HEAD, HEAD), jnp.int32),
            pltpu.VMEM((FRESH // HEAD, HEAD), jnp.int32),
            pltpu.VMEM((n, 2, CAP, HEAD), BF16),
            pltpu.VMEM((wide, SEQ), F32),
            pltpu.VMEM((wide, FRESH), F32),
            pltpu.VMEM((wide, SEQ), BF16),
            pltpu.VMEM((wide, FRESH), BF16),
            pltpu.VMEM((wide, HEAD), F32),
            pltpu.VMEM((SIDE, wide // SIDE + 2 * GROUP, HEAD), BF16),
            pltpu.VMEM((n, wide // SIDE + 2 * GROUP, HEAD), BF16),
            pltpu.VMEM((SIDE, wide // SIDE, HEAD), BF16),
            pltpu.VMEM((2, SIDE, ROWS // 2, HEAD), F32),
            pltpu.VMEM((SIDE, ROWS // 2, HEAD), F32),
            pltpu.VMEM((SIDE, ROWS // 2, HEAD), F32),
            pltpu.VMEM((SIDE, ROWS // 2, HEAD), F32),
            dma((7,)),
            dma((steps,)),
            dma((steps,)),
            dma,
        ]
        + [dma((n,))] * 4
        + [dma((SIDE,))] * 4,
        compiler_params=pltpu.CompilerParams(
            collective_id=0, has_side_effects=True, vmem_limit_bytes=60 << 20
        ),
        name="decode",
    )(
        queries,
        cache_keys,
        cache_values,
        lengths,
        new_keys,
        new_values,
        new_rows.reshape(FRESH // HEAD, HEAD),
        owners.reshape(FRESH // HEAD, HEAD),
        out_weight,
    )
    return pl.pallas_call(
        finish,
        out_shape=shapes,
        in_specs=[vmem_space] * 2,
        out_specs=(any_space, any_space),
        scratch_shapes=[dma((2,))],
        compiler_params=pltpu.CompilerParams(vmem_limit_bytes=60 << 20),
        name="finish",
    )(*(pltpu.with_memory_space_constraint(one, pltpu.VMEM) for one in made))


def solution(mesh):
    placed = (
        P(None, "tp"),
        P(None, "grp", "tp"),
        P(None, "grp", "tp"),
        P(),
        P("grp", "tp"),
        P("grp", "tp"),
        P("grp"),
        P("grp", None),
        P("tp", "grp"),
    )
    return jax.shard_map(
        functools.partial(on_device, mesh.shape["grp"], mesh.shape["tp"]),
        mesh=mesh,
        in_specs=placed,
        out_specs=(P(None, ("grp", "tp")), P(None, "grp", "tp")),
        check_vma=False,
    )
```
